256 devices in a mesh: gx: 4 (over x), gy: 8 (over y, core), gz: 8 (over z).
Axes of the slice: x: 4, y: 4, z: 8, core: 2. Of those that a mesh axis runs over, the one named last changes fastest.
Arguments:
- panel: float32 [4, 8, 32, 256, 256], P('gx', 'gy', 'gz'), may hold values from -120 to 120
- tiles: float32 [4, 8, 32, 10, 256, 256], P('gx', 'gy', 'gz'), may hold values from -0.125 to 0.125
- codes: int32 [4, 8, 32, 10], P('gx', 'gy', 'gz'), may hold values from 0 to 26, as said below
Outputs:
- bands: float32 [4, 8, 32, 256, 256], P('gx', 'gy', 'gz')
- factor: float32 [256, 256], replicated
The draws below stay inside these ranges and needn't reach their ends.
Inputs may be any that keep to these rules, and one draw needn't show every extreme that they name: Slot 0 of every element holds 13, the element itself; the other 9 slots of an element hold distinct codes other than 13.
All inputs are finite; a program needn't handle non-finite values.
Results may differ from the reference program's by a relative error of at most 0.0003.
Values sent between devices are 32-bit elements; how exact they have to be, the bound alone decides.
No kernel may reach another device: no remote copies, remote signals or barrier semaphores. Data moves between devices by JAX's collectives and lax.ppermute only.
A program may use at most 128 MiB of HBM per device.

```python
import math
import jax
import jax.numpy as jnp
from jax import lax

BASIS_PER_ELEM = 256
BAND_COUNT = 256
TILE_SLOTS = 10
ELEMENTS_X = 4
ELEMENTS_Y = 8
ELEMENTS_Z = 32


def draw_codes(key, part):
    grand_total = ELEMENTS_X * ELEMENTS_Y * ELEMENTS_Z

    def element_cell(index):
        order = jax.random.permutation(jax.random.fold_in(key, index), 26).astype(jnp.int32)
        others = order[:TILE_SLOTS - 1]
        others = others + (others >= 13).astype(jnp.int32)
        return jnp.concatenate([jnp.full((1,), 13, jnp.int32), others])
    return jax.vmap(element_cell)(jnp.arange(grand_total, dtype=jnp.int32)).reshape(ELEMENTS_X, ELEMENTS_Y, ELEMENTS_Z, TILE_SLOTS)


def draw_panel(key, part):
    panel_random_key = jax.random.split(jax.random.fold_in(key, 7), 5)
    array_shape = (ELEMENTS_X, ELEMENTS_Y, ELEMENTS_Z, BASIS_PER_ELEM, BAND_COUNT)
    common_shape = (ELEMENTS_X, ELEMENTS_Y, ELEMENTS_Z, BASIS_PER_ELEM, 4)
    base = jnp.clip(jax.random.normal(panel_random_key[2], array_shape, jnp.float32), -4.0, 4.0)
    shared = jnp.clip(jax.random.normal(panel_random_key[3], common_shape, jnp.float32), -4.0, 4.0)
    element_scale_factor = jnp.exp(jax.random.uniform(panel_random_key[0], (ELEMENTS_X, ELEMENTS_Y, ELEMENTS_Z, 1, 1), jnp.float32) * math.log(10.0))
    mixing = jax.random.uniform(panel_random_key[4], (4, BAND_COUNT), jnp.float32, -1.5, 1.5)
    combined = base
    for component in range(4):
        combined = combined + 0.3 * shared[..., component:component + 1] * mixing[component]
    combined = combined / 2.8
    band_scale = 0.3 * jnp.exp(jax.random.uniform(panel_random_key[1], (1, 1, 1, 1, BAND_COUNT), jnp.float32) * math.log(10.0))
    return combined * element_scale_factor * band_scale


def levels(own_key, dims, shards, low, top_value):
    def one(axis_at, parts):
        draws = jax.random.uniform(jax.random.fold_in(jax.random.fold_in(own_key, 6), axis_at), (parts,), jnp.float32, low / len(shards), top_value / len(shards))
        return jnp.repeat(jnp.exp(draws), dims[axis_at] // parts).reshape((-1,) + (1,) * (len(dims) - axis_at - 1))

    factor_of = one(*shards[0])
    for cut in shards[1:]:
        factor_of = factor_of * one(*cut)
    return factor_of


def normal_values(rng, shape, scale, limit, pieces=(), kind=jnp.bfloat16):
    values = jax.random.normal(rng, shape, jnp.float32) * scale
    if len(pieces) > 0:
        values = levels(rng, shape, pieces, -0.22, 0.18) * values
    return jnp.clip(values, min=-limit, max=limit).astype(kind)


def setup_inputs(seed: int = 0) -> dict:
    key_list = jax.random.split(jax.random.key(seed), 4)
    return {
        "panel": draw_panel(jax.random.fold_in(key_list[3], 71), 0),
        "tiles": normal_values(key_list[1], (ELEMENTS_X, ELEMENTS_Y, ELEMENTS_Z, TILE_SLOTS, BASIS_PER_ELEM, BASIS_PER_ELEM), (BASIS_PER_ELEM * TILE_SLOTS) ** -0.5, 0.125, ((0, 4), (1, 8), (2, 8)), jnp.float32),
        "codes": draw_codes(jax.random.fold_in(key_list[3], 71), 0),
    }


def reference(panel, tiles, codes):
    grid_y = panel.shape[1]
    grid_z = panel.shape[2]
    grand_total = panel.shape[0] * grid_y * grid_z
    padded = jnp.pad(panel, ((1, 1), (1, 1), (1, 1), (0, 0), (0, 0)))
    basis = panel.shape[3]
    width = panel.shape[4]

    def window(first, second, third):
        zero = jnp.zeros((), jnp.int32)
        piece = lax.dynamic_slice(padded, (first.astype(jnp.int32), second.astype(jnp.int32), third.astype(jnp.int32), zero, zero), (1, 1, 1, basis, width))
        return piece[0, 0, 0]

    def element_cell(flat):
        x_index = flat // (grid_y * grid_z)
        y_index = flat // grid_z % grid_y
        z_index = flat % grid_z
        slot_codes = codes[x_index, y_index, z_index]
        windows = jax.vmap(lambda c: window(x_index + c // 9, y_index + c // 3 % 3, z_index + c % 3))(slot_codes)
        applied = jnp.einsum('kab,kbc->ac', tiles[x_index, y_index, z_index], windows, precision=lax.Precision.HIGHEST)
        return applied - 0.5 * panel[x_index, y_index, z_index]
    filtered = lax.map(element_cell, jnp.arange(grand_total, dtype=jnp.int32))
    flat_rows = filtered.reshape(-1, width)
    gram = jnp.dot(flat_rows.T, flat_rows, precision=lax.Precision.HIGHEST) / flat_rows.shape[0]
    lower = jnp.linalg.cholesky(gram)
    inverse = lax.linalg.triangular_solve(lower, jnp.eye(width, dtype=gram.dtype), left_side=True, lower=True)
    bands = jnp.dot(flat_rows, inverse.T, precision=lax.Precision.HIGHEST).reshape(panel.shape)
    return (bands, lower.T)
```

```python
import functools

import jax
import jax.numpy as jnp
import numpy as np
from jax import lax
from jax.experimental import pallas as pl
from jax.experimental.pallas import tpu as pltpu
from jax.sharding import PartitionSpec as P

F32 = jnp.float32
BF16 = jnp.bfloat16
EXACT = lax.Precision.HIGHEST
CELLS = 4
SLOTS = 10
SIDE = 256
BLOCK = 64

EARLY = (
    ("own", 4), ("o", 4), ("i", 4), ("below", 1), ("above", 1), ("ends-", 2), ("ends+", 2),
    ("mids-", 2), ("mids+", 2), ("o_ends", 4), ("below2", 3), ("above2", 3), ("i2", 6),
)
LATE = (("o_mids", 4), ("below3", 2), ("above3", 2), ("i3", 8))


def place(column, dx, z):
    side = int(dx > 0)
    sign = "+" if dx > 0 else "-"
    last = int(z == CELLS - 1)
    inside = 0 <= z < CELLS
    mid = z in (1, 2)
    outer = "below" if z < 0 else "above"
    if column == "own":
        if dx == 0:
            return ("own", z) if inside else (outer, 0)
        if inside:
            return ("mids" + sign, z - 1) if mid else ("ends" + sign, last)
        return (outer + "2", side)
    if column == "o":
        if dx == 0:
            return ("o", z) if inside else (outer + "2", 2)
        if inside:
            return ("o_mids", 2 * side + z - 1) if mid else ("o_ends", 2 * side + last)
        return (outer + "3", side)
    if dx == 0:
        return ("i", z) if inside else ("i2", 4 + int(z > 0))
    if inside:
        return ("i3", 2 * side + z - 1) if mid else ("i2", 2 * side + last)
    return ("i3", 4 + 2 * int(z > 0) + side)


def lookup(buffers):
    start, total = {}, 0
    for name, count in buffers:
        start[name] = total
        total += count
    table = np.full((2, CELLS, 27), -1, np.int32)
    for parity in range(2):
        for cell in range(CELLS):
            for code in range(27):
                dx, dy, dz = code // 9 - 1, code // 3 % 3 - 1, code % 3 - 1
                inner = 1 if parity == 0 else -1
                column = "own" if dy == 0 else "i" if dy == inner else "o"
                name, at = place(column, dx, cell + dz)
                if name in start:
                    table[parity, cell, code] = start[name] + at
    return table.reshape(2, CELLS * 27), total


def split(values):
    high = values.astype(BF16)
    return high, (values - high.astype(F32)).astype(BF16)


def product(a, b):
    ah, al = split(a)
    bh, bl = split(b)
    return jnp.dot(
        jnp.concatenate([ah, ah, al], axis=1),
        jnp.concatenate([bh, bl, bh], axis=0),
        preferred_element_type=F32,
    )


def apply_kernel(counts, first, table_ref, codes_ref, tiles_ref, *rest):
    buffers, rest = rest[: len(counts)], rest[len(counts) :]
    if first:
        out_ref, window, tile, window_sem, tile_sem = rest
    else:
        before_ref, out_ref, gram_ref, window, tile, window_sem, tile_sem = rest

    def entry(at):
        return table_ref[at // SLOTS * 27 + codes_ref[at]]

    copies, start = [], 0
    for n, (count, ref) in enumerate(zip(counts, buffers)):
        copy = pltpu.make_async_copy(ref, window.at[pl.ds(start, count)], window_sem.at[n])
        copy.start()
        copies.append(copy)
        start += count

    def fetch(at):
        return pltpu.make_async_copy(tiles_ref.at[at], tile.at[at], tile_sem.at[at])

    def begin(at, carry):
        @pl.when(entry(at) >= 0)
        def _():
            fetch(at).start()

        return carry

    lax.fori_loop(0, CELLS * SLOTS, begin, 0)
    for copy in copies:
        copy.wait()
    for cell in range(CELLS):
        out_ref[cell] = -0.5 * window[cell] if first else before_ref[cell]

    def slot(at, carry):
        e = entry(at)

        @pl.when(e >= 0)
        def _():
            fetch(at).wait()
            cell = at // SLOTS
            out_ref[cell] += product(tile[at], window[e])

        return carry

    lax.fori_loop(0, CELLS * SLOTS, slot, 0)
    if not first:
        gram = jnp.zeros((SIDE, SIDE), F32)
        for cell in range(CELLS):
            high, low = split(out_ref[cell])
            gram += lax.dot_general(
                jnp.concatenate([high, high, low], axis=0),
                jnp.concatenate([high, low, high], axis=0),
                (((0,), (0,)), ((), ())),
                preferred_element_type=F32,
            )
        half = SIDE // 2
        gram_ref[:half] = gram[:half, :half]
        gram_ref[half : 2 * half] = gram[:half, half:]
        gram_ref[2 * half :] = gram[half:, half:]


def apply(names, table, codes, tiles, buffers, before=None):
    counts = tuple(count for _, count in names)
    first = before is None
    smem = pl.BlockSpec(memory_space=pltpu.SMEM)
    anywhere = pl.BlockSpec(memory_space=pl.ANY)
    vmem = pl.BlockSpec(memory_space=pltpu.VMEM)
    panel = jax.ShapeDtypeStruct((CELLS, SIDE, SIDE), F32)
    packed = jax.ShapeDtypeStruct((3 * SIDE // 2, SIDE // 2), F32)
    return pl.pallas_call(
        functools.partial(apply_kernel, counts, first),
        out_shape=panel if first else (panel, packed),
        in_specs=[smem, smem, anywhere] + [anywhere] * len(counts) + ([] if first else [vmem]),
        out_specs=vmem if first else (vmem, vmem),
        scratch_shapes=[
            pltpu.VMEM((sum(counts), SIDE, SIDE), F32),
            pltpu.VMEM((CELLS * SLOTS, SIDE, SIDE), F32),
            pltpu.SemaphoreType.DMA((len(counts),)),
            pltpu.SemaphoreType.DMA((CELLS * SLOTS,)),
        ],
        compiler_params=pltpu.CompilerParams(vmem_limit_bytes=40 << 20),
        cost_estimate=pl.CostEstimate(
            flops=(30 if first else 10) * 2 * 3 * SIDE**3, bytes_accessed=16 << 20, transcendentals=0
        ),
        name="apply_early" if first else "apply_late",
    )(table, codes, tiles, *buffers, *(() if first else (before,)))


def leaf(rows):
    rows = list(rows)
    at = lax.broadcasted_iota(jnp.int32, (8, 128), 0)
    count = len(rows)
    for b in range(count):
        rest = range(b, count)
        column = {
            (k, v): jnp.broadcast_to(rows[v][:, 8 * b + k : 8 * b + k + 1], (8, 128))
            for k in range(8)
            for v in rest
        }
        for j in range(8):
            scale = lax.rsqrt(jnp.broadcast_to(column[j, b][j : j + 1], (8, 128)))
            times = {v: column[j, v] * scale for v in rest}
            times[b] = jnp.where(at > j, times[b], 0.0)
            for k in range(j + 1, 8):
                pivot = jnp.broadcast_to(column[k, b][j : j + 1], (8, 128)) * scale
                for v in rest:
                    column[k, v] = column[k, v] - times[v] * pivot
            pivot = jnp.broadcast_to(rows[b][j : j + 1], (8, 128)) * scale
            for v in rest:
                if v > b:
                    rows[v] = rows[v] - times[v] * pivot
            rows[b] = jnp.where(at == j, pivot, rows[b] - times[b] * pivot)
    return rows


def factor_kernel(total, gram_ref, filtered_ref, bands_ref, factor_ref, work):
    half = SIDE // 2
    row = lax.broadcasted_iota(jnp.int32, (SIDE, SIDE), 0)
    col = lax.broadcasted_iota(jnp.int32, (SIDE, SIDE), 1)
    work[:half, :half] = gram_ref[:half] * (1.0 / total)
    work[:half, half:SIDE] = gram_ref[half : 2 * half] * (1.0 / total)
    work[half:, :half] = jnp.zeros((half, half), F32)
    work[half:, half:SIDE] = gram_ref[2 * half :] * (1.0 / total)
    work[:, SIDE:] = (row == col).astype(F32)
    eye = (row == col)[:BLOCK, :BLOCK].astype(F32)
    for low in range(0, SIDE, BLOCK):
        high = low + BLOCK
        rows = pl.ds(low, BLOCK)
        block = jnp.concatenate([work[rows, low:high], eye], axis=1)
        done = jnp.concatenate(leaf([block[8 * v : 8 * v + 8] for v in range(BLOCK // 8)]), axis=0)
        solved = jnp.dot(done[:, BLOCK:], work[rows, :], precision=EXACT, preferred_element_type=F32)
        work[rows, :] = solved
        if high < SIDE:
            under = pl.ds(high, SIDE - high)
            work[under, :] = work[under, :] - lax.dot_general(
                solved[:, high:SIDE],
                solved,
                (((0,), (0,)), ((), ())),
                precision=EXACT,
                preferred_element_type=F32,
            )
    factor_ref[...] = jnp.where(row <= col, work[:, :SIDE], 0.0)
    high, low = split(jnp.where(row >= col, work[:, SIDE:], 0.0))
    right = jnp.concatenate([high, low, high], axis=1)
    for cell in range(CELLS):
        fh, fl = split(filtered_ref[cell])
        bands_ref[cell] = lax.dot_general(
            jnp.concatenate([fh, fh, fl], axis=1),
            right,
            (((1,), (1,)), ((), ())),
            preferred_element_type=F32,
        )


def factorise(gram, filtered, total):
    vmem = pl.BlockSpec(memory_space=pltpu.VMEM)
    return pl.pallas_call(
        functools.partial(factor_kernel, total),
        out_shape=(
            jax.ShapeDtypeStruct((CELLS, SIDE, SIDE), F32),
            jax.ShapeDtypeStruct((SIDE, SIDE), F32),
        ),
        in_specs=[vmem, vmem],
        out_specs=(vmem, vmem),
        scratch_shapes=[pltpu.VMEM((SIDE, 2 * SIDE), F32)],
        compiler_params=pltpu.CompilerParams(vmem_limit_bytes=32 << 20),
        name="factorise",
    )(gram, filtered)


def flip(values, axis, bit):
    size = lax.axis_size(axis)
    return lax.ppermute(values, axis, [(i, i ^ bit) for i in range(size)])


def summed(values):
    halved = (("gy", 1), ("gx", 1), ("gx", 2))
    for axis, bit in halved:
        half = values.shape[0] // 2
        upper = (lax.axis_index(axis) // bit) % 2 == 1
        a, b = values[:half], values[half:]
        values = jnp.where(upper, b, a) + flip(jnp.where(upper, a, b), axis, bit)
    for axis, bit in (("gy", 2), ("gy", 4), ("gz", 1), ("gz", 2), ("gz", 4)):
        values = values + flip(values, axis, bit)
    for axis, bit in halved[::-1]:
        upper = (lax.axis_index(axis) // bit) % 2 == 1
        other = flip(values, axis, bit)
        values = jnp.concatenate(
            [jnp.where(upper, other, values), jnp.where(upper, values, other)], axis=0
        )
    return values


def up(values, axis):
    return lax.ppermute(values, axis, [(i, i + 1) for i in range(lax.axis_size(axis) - 1)])


def down(values, axis):
    return lax.ppermute(values, axis, [(i + 1, i) for i in range(lax.axis_size(axis) - 1)])


def across(values):
    size = lax.axis_size("gy")
    pairs = [(i, i + 1) for i in range(1, size - 1, 2)]
    return lax.ppermute(values, "gy", pairs + [(j, i) for i, j in pairs])


def per_device(panel, tiles, codes):
    own = panel[0, 0]
    ends = jnp.concatenate([own[:1], own[CELLS - 1 :]], axis=0)
    mids = own[1:3]
    got = {"own": own}
    got["ends-"], got["ends+"] = up(ends, "gx"), down(ends, "gx")
    got["o"] = across(own)
    got["below"], got["above"] = up(own[CELLS - 1 :], "gz"), down(own[:1], "gz")
    got["i"] = flip(own, "gy", 1)

    sides = jnp.concatenate([got["ends-"], got["ends+"]], axis=0)
    got["o_ends"] = across(sides)
    tops = jnp.concatenate([sides[1:2], sides[3:], got["o"][CELLS - 1 :]], axis=0)
    bottoms = jnp.concatenate([sides[:1], sides[2:3], got["o"][:1]], axis=0)
    got["below2"], got["above2"] = up(tops, "gz"), down(bottoms, "gz")
    got["mids-"], got["mids+"] = up(mids, "gx"), down(mids, "gx")
    got["i2"] = flip(jnp.concatenate([sides, got["below"], got["above"]], axis=0), "gy", 1)

    middle = jnp.concatenate([got["mids-"], got["mids+"]], axis=0)
    got["o_mids"] = across(middle)
    o_ends = got["o_ends"]
    got["below3"] = up(jnp.concatenate([o_ends[1:2], o_ends[3:]], axis=0), "gz")
    got["above3"] = down(jnp.concatenate([o_ends[:1], o_ends[2:3]], axis=0), "gz")
    got["i3"] = flip(
        jnp.concatenate([middle, got["below2"][:2], got["above2"][:2]], axis=0), "gy", 1
    )

    odd = lax.axis_index("gy") % 2 == 1
    flat_tiles = tiles.reshape(CELLS * SLOTS, SIDE, SIDE)
    flat_codes = codes.reshape(CELLS * SLOTS)
    filtered = None
    for names in (EARLY, LATE):
        table, _ = lookup(names)
        chosen = jnp.where(odd, jnp.asarray(table[1]), jnp.asarray(table[0]))
        filtered = apply(
            names, chosen, flat_codes, flat_tiles, [got[name] for name, _ in names], filtered
        )
    filtered, gram = filtered
    devices = lax.axis_size("gx") * lax.axis_size("gy") * lax.axis_size("gz")
    bands, factor = factorise(summed(gram), filtered, CELLS * SIDE * devices)
    return bands.reshape(panel.shape), factor


def solution(mesh):
    in_specs = (
        P("gx", "gy", "gz", None, None),
        P("gx", "gy", "gz", None, None, None),
        P("gx", "gy", "gz", None),
    )
    out_specs = (P("gx", "gy", "gz", None, None), P())
    return jax.shard_map(
        per_device, mesh=mesh, in_specs=in_specs, out_specs=out_specs, check_vma=False
    )
```

```python
import functools

import jax
import jax.numpy as jnp
import numpy as np
from jax import lax
from jax.experimental import pallas as pl
from jax.experimental.pallas import tpu as pltpu
from jax.sharding import PartitionSpec as P

F32 = jnp.float32
BF16 = jnp.bfloat16
EXACT = lax.Precision.HIGHEST
CELLS = 4
SLOTS = 10
SIDE = 256
GROUP = 4
ROOM = 48
BLOCK = 64

STAGES = (
    (
        ("own", 4), ("o", 4), ("i", 4), ("ends-", 2), ("ends+", 2),
        ("mids-", 2), ("mids+", 2), ("o2", 4), ("below2", 3), ("above2", 3),
    ),
    (("o3", 6), ("below3", 2), ("above3", 2), ("i3", 14)),
)


def place(column, dx, z):
    side = int(dx > 0)
    sign = "+" if dx > 0 else "-"
    last = int(z == CELLS - 1)
    inside = 0 <= z < CELLS
    mid = z in (1, 2)
    above = int(z > 0)
    outer = "above" if above else "below"
    if column == "own":
        if not inside:
            return (outer + "2", 0 if dx == 0 else 1 + side)
        if dx == 0:
            return ("own", z)
        return ("mids" + sign, z - 1) if mid else ("ends" + sign, last)
    if inside:
        if dx == 0:
            return (column, z)
        if mid:
            return (column + "3", 2 * side + z - 1)
        return ("o2", 2 * side + last) if column == "o" else ("i3", 10 + 2 * side + last)
    if column == "o":
        return ("o3", 4 + above) if dx == 0 else (outer + "3", side)
    return ("i3", 4 + 3 * above + (0 if dx == 0 else 1 + side))


def lookup(buffers):
    start, total = {}, 0
    for name, count in buffers:
        start[name] = total
        total += count
    table = np.full((2, CELLS, 27), -1, np.int32)
    for parity in range(2):
        for cell in range(CELLS):
            for code in range(27):
                dx, dy, dz = code // 9 - 1, code // 3 % 3 - 1, code % 3 - 1
                inner = 1 if parity == 0 else -1
                column = "own" if dy == 0 else "i" if dy == inner else "o"
                name, at = place(column, dx, cell + dz)
                if name in start:
                    table[parity, cell, code] = start[name] + at
    return table.reshape(2, CELLS * 27)


def split(values):
    high = values.astype(BF16)
    return high, (values - high.astype(F32)).astype(BF16)


def product(a, b):
    ah, al = split(a)
    bh, bl = split(b)
    return jnp.dot(
        jnp.concatenate([ah, ah, al], axis=1),
        jnp.concatenate([bh, bl, bh], axis=0),
        preferred_element_type=F32,
    )


def pack_kernel(pieces, taken, given, *refs):
    sources, outs, sem = refs[:taken], refs[given:-1], refs[-1]
    copies = []
    for out, parts in zip(outs, pieces):
        start = 0
        for source, low, count in parts:
            copy = pltpu.make_async_copy(
                sources[source].at[pl.ds(low, count)],
                out.at[pl.ds(start, count)],
                sem.at[len(copies)],
            )
            copy.start()
            copies.append(copy)
            start += count
    for copy in copies:
        copy.wait()


def pack(got, payloads, after=()):
    names = sorted({name for parts in payloads for name, _, _ in parts})
    pieces = [[(names.index(name), low, count) for name, low, count in parts] for parts in payloads]
    anywhere = pl.BlockSpec(memory_space=pl.ANY)
    return pl.pallas_call(
        functools.partial(pack_kernel, pieces, len(names), len(names) + len(after)),
        out_shape=tuple(
            jax.ShapeDtypeStruct((sum(count for _, _, count in parts), SIDE, SIDE), F32)
            for parts in payloads
        ),
        in_specs=[anywhere] * (len(names) + len(after)),
        out_specs=(anywhere,) * len(payloads),
        scratch_shapes=[pltpu.SemaphoreType.DMA((sum(map(len, payloads)),))],
        compiler_params=pltpu.CompilerParams(vmem_limit_bytes=1 << 20),
        name="pack",
    )(*(got[name] for name in names), *after)


def listed(table_ref, codes_ref, chosen, begin):
    taken = jnp.int32(0)
    for cell in range(CELLS):
        for at in range(cell * SLOTS, (cell + 1) * SLOTS):
            entry = table_ref[27 * cell + codes_ref[at]]

            @pl.when(entry >= 0)
            def _(at=at, cell=cell, entry=entry, taken=taken):
                chosen[0, taken] = jnp.int32(at)
                chosen[1, taken] = entry
                chosen[2, taken] = jnp.int32(cell)
                begin(at, taken)

            taken = taken + (entry >= 0).astype(jnp.int32)
    return taken


def multiply(taken, chosen, tile, window, arrived, total):
    for n in range(GROUP - 1):
        chosen[1, taken + n] = jnp.int32(0)
        chosen[2, taken + n] = jnp.int32(0)
        tile[taken + n] = jnp.zeros((SIDE, SIDE), F32)

    def group(g, carry):
        first = GROUP * g
        for n in range(GROUP):

            @pl.when(first + n < taken)
            def _(n=first + n):
                arrived(n)

        done = [product(tile[first + n], window[chosen[1, first + n]]) for n in range(GROUP)]
        for n in range(GROUP):
            total[chosen[2, first + n]] += done[n]
        return carry

    lax.fori_loop(0, (taken + GROUP - 1) // GROUP, group, 0)


def early_kernel(counts, table_ref, later_ref, codes_ref, tiles_ref, *rest):
    buffers, rest = rest[: len(counts)], rest[len(counts) :]
    out_ref, list_ref, window, tile, chosen, window_sem, tile_sem = rest
    copies, start = [], 0
    for n, (count, ref) in enumerate(zip(counts, buffers)):
        copy = pltpu.make_async_copy(ref, window.at[pl.ds(start, count)], window_sem.at[n])
        copy.start()
        copies.append(copy)
        start += count

    def fetch(at, n):
        return pltpu.make_async_copy(tiles_ref.at[at], tile.at[n], tile_sem.at[n])

    taken = listed(table_ref, codes_ref, chosen, lambda at, n: fetch(at, n).start())
    list_ref[0, ROOM - 1] = listed(later_ref, codes_ref, list_ref, lambda at, n: None)
    for copy in copies:
        copy.wait()
    for cell in range(CELLS):
        out_ref[cell] = -0.5 * window[cell]
    multiply(taken, chosen, tile, window, lambda n: fetch(0, n).wait(), out_ref)


def late_kernel(counts, list_ref, tiles_ref, before_ref, *rest):
    buffers, rest = rest[: len(counts)], rest[len(counts) :]
    out_ref, gram_ref, total, window, tile, chosen, window_sem, tile_sem, sems = rest
    taken = list_ref[0, ROOM - 1]

    def fetch(at, n):
        return pltpu.make_async_copy(tiles_ref.at[at], tile.at[n], tile_sem.at[n])

    def begin(n, carry):
        entry = list_ref[1, n]
        chosen[1, n] = n
        chosen[2, n] = list_ref[2, n]
        fetch(list_ref[0, n], n).start()
        start = 0
        for count, ref in zip(counts, buffers):

            @pl.when((entry >= start) & (entry < start + count))
            def _(ref=ref, start=start):
                pltpu.make_async_copy(ref.at[entry - start], window.at[n], window_sem.at[n]).start()

            start += count
        return carry

    def arrived(n):
        fetch(0, n).wait()
        pltpu.make_async_copy(buffers[0].at[0], window.at[n], window_sem.at[n]).wait()

    lax.fori_loop(0, taken, begin, 0)
    before = pltpu.make_async_copy(before_ref, total, sems.at[CELLS])
    before.start()
    before.wait()
    multiply(taken, chosen, tile, window, arrived, total)
    copies = [
        pltpu.make_async_copy(total.at[cell], out_ref.at[cell], sems.at[cell]) for cell in range(CELLS)
    ]
    for copy in copies:
        copy.start()
    gram = jnp.zeros((SIDE, SIDE), F32)
    for cell in range(CELLS):
        high, low = split(total[cell])
        gram += lax.dot_general(
            jnp.concatenate([high, high, low], axis=0),
            jnp.concatenate([high, low, high], axis=0),
            (((0,), (0,)), ((), ())),
            preferred_element_type=F32,
        )
    gram_ref[...] = gram
    for copy in copies:
        copy.wait()


SMEM = pl.BlockSpec(memory_space=pltpu.SMEM)
FAR = pl.BlockSpec(memory_space=pltpu.HBM)
NEAR = pl.BlockSpec(memory_space=pltpu.VMEM)
SLOT_ROOM = CELLS * SLOTS + GROUP


def apply(odd, codes, tiles, got):
    early, late = STAGES
    tables = [jnp.where(odd, jnp.asarray(t[1]), jnp.asarray(t[0])) for t in map(lookup, STAGES)]
    counts = tuple(count for _, count in early)
    panel = jax.ShapeDtypeStruct((CELLS, SIDE, SIDE), F32)
    chosen = pltpu.SMEM((3, SLOT_ROOM), jnp.int32)
    tile = pltpu.VMEM((SLOT_ROOM, SIDE, SIDE), F32)
    params = pltpu.CompilerParams(vmem_limit_bytes=60 << 20)
    cost = pl.CostEstimate(
        flops=SLOTS * CELLS * 2 * SIDE**3, bytes_accessed=12 << 20, transcendentals=0
    )
    part, left = pl.pallas_call(
        functools.partial(early_kernel, counts),
        out_shape=(panel, jax.ShapeDtypeStruct((3, ROOM), jnp.int32)),
        in_specs=[SMEM, SMEM, SMEM, FAR] + [FAR] * len(counts),
        out_specs=(NEAR, SMEM),
        scratch_shapes=[
            pltpu.VMEM((sum(counts), SIDE, SIDE), F32),
            tile,
            chosen,
            pltpu.SemaphoreType.DMA((len(counts),)),
            pltpu.SemaphoreType.DMA((SLOT_ROOM,)),
        ],
        compiler_params=params,
        cost_estimate=cost,
        name="apply_early",
    )(*tables, codes, tiles, *(got[name] for name, _ in early))
    counts = tuple(count for _, count in late)
    return pl.pallas_call(
        functools.partial(late_kernel, counts),
        out_shape=(panel, jax.ShapeDtypeStruct((SIDE, SIDE), F32)),
        in_specs=[SMEM, FAR, FAR] + [FAR] * len(counts),
        out_specs=(FAR, NEAR),
        scratch_shapes=[
            pltpu.VMEM((CELLS, SIDE, SIDE), F32),
            tile,
            tile,
            chosen,
            pltpu.SemaphoreType.DMA((SLOT_ROOM,)),
            pltpu.SemaphoreType.DMA((SLOT_ROOM,)),
            pltpu.SemaphoreType.DMA((CELLS + 1,)),
        ],
        compiler_params=params,
        cost_estimate=cost,
        name="apply_late",
    )(left, tiles, part, *(got[name] for name, _ in late))


def leaf(rows):
    rows = list(rows)
    at = lax.broadcasted_iota(jnp.int32, (8, 128), 0)
    count = len(rows)
    for b in range(count):
        rest = range(b, count)
        column = {
            (k, v): jnp.broadcast_to(rows[v][:, 8 * b + k : 8 * b + k + 1], (8, 128))
            for k in range(8)
            for v in rest
        }
        for j in range(8):
            scale = lax.rsqrt(jnp.broadcast_to(column[j, b][j : j + 1], (8, 128)))
            times = {v: column[j, v] * scale for v in rest}
            times[b] = jnp.where(at > j, times[b], 0.0)
            for k in range(j + 1, 8):
                pivot = jnp.broadcast_to(column[k, b][j : j + 1], (8, 128)) * scale
                for v in rest:
                    column[k, v] = column[k, v] - times[v] * pivot
            pivot = jnp.broadcast_to(rows[b][j : j + 1], (8, 128)) * scale
            for v in rest:
                if v > b:
                    rows[v] = rows[v] - times[v] * pivot
            rows[b] = jnp.where(at == j, pivot, rows[b] - times[b] * pivot)
    return rows


def factor_kernel(total, gram_ref, filtered_ref, bands_ref, factor_ref, work, filtered, bands, sems):
    fetch = pltpu.make_async_copy(filtered_ref, filtered, sems.at[CELLS])
    fetch.start()
    row = lax.broadcasted_iota(jnp.int32, (SIDE, SIDE), 0)
    col = lax.broadcasted_iota(jnp.int32, (SIDE, SIDE), 1)
    work[:, :SIDE] = gram_ref[...] * (1.0 / total)
    work[:, SIDE:] = (row == col).astype(F32)
    eye = (row == col)[:BLOCK, :BLOCK].astype(F32)
    for low in range(0, SIDE, BLOCK):
        high = low + BLOCK
        rows = pl.ds(low, BLOCK)
        block = jnp.concatenate([work[rows, low:high], eye], axis=1)
        done = jnp.concatenate(leaf([block[8 * v : 8 * v + 8] for v in range(BLOCK // 8)]), axis=0)
        solved = jnp.dot(done[:, BLOCK:], work[rows, :], precision=EXACT, preferred_element_type=F32)
        work[rows, :] = solved
        if high < SIDE:
            under = pl.ds(high, SIDE - high)
            work[under, :] = work[under, :] - lax.dot_general(
                solved[:, high:SIDE],
                solved,
                (((0,), (0,)), ((), ())),
                precision=EXACT,
                preferred_element_type=F32,
            )
    factor_ref[...] = jnp.where(row <= col, work[:, :SIDE], 0.0)
    high, low = split(jnp.where(row >= col, work[:, SIDE:], 0.0))
    right = jnp.concatenate([high, low, high], axis=1)
    fetch.wait()
    copies = []
    for cell in range(CELLS):
        fh, fl = split(filtered[cell])
        bands[cell] = lax.dot_general(
            jnp.concatenate([fh, fh, fl], axis=1),
            right,
            (((1,), (1,)), ((), ())),
            preferred_element_type=F32,
        )
        copies.append(pltpu.make_async_copy(bands.at[cell], bands_ref.at[cell], sems.at[cell]))
        copies[cell].start()
    for copy in copies:
        copy.wait()


def factorise(gram, filtered, total):
    vmem = pl.BlockSpec(memory_space=pltpu.VMEM)
    far = pl.BlockSpec(memory_space=pltpu.HBM)
    panel = (CELLS, SIDE, SIDE)
    return pl.pallas_call(
        functools.partial(factor_kernel, total),
        out_shape=(jax.ShapeDtypeStruct(panel, F32), jax.ShapeDtypeStruct((SIDE, SIDE), F32)),
        in_specs=[vmem, far],
        out_specs=(far, vmem),
        scratch_shapes=[
            pltpu.VMEM((SIDE, 2 * SIDE), F32),
            pltpu.VMEM(panel, F32),
            pltpu.VMEM(panel, F32),
            pltpu.SemaphoreType.DMA((CELLS + 1,)),
        ],
        compiler_params=pltpu.CompilerParams(vmem_limit_bytes=62_488_000),
        name="factorise",
    )(gram, filtered)


def flip(values, axis, bit):
    size = lax.axis_size(axis)
    return lax.ppermute(values, axis, [(i, i ^ bit) for i in range(size)])


def exchange(pieces, axes):
    return lax.all_to_all(pieces, axes, 0, 0).reshape(pieces.shape)


def summed(gram):
    plane = ("gx", "gy")
    peers, planes = lax.axis_size("gx") * lax.axis_size("gy"), lax.axis_size("gz")
    rows = exchange(gram.reshape(peers, SIDE // peers, SIDE), plane).sum(0)
    rows = exchange(jnp.broadcast_to(rows, (planes, *rows.shape)), "gz").sum(0)
    return exchange(jnp.broadcast_to(rows, (peers, *rows.shape)), plane).reshape(SIDE, SIDE)


def up(values, axis):
    return lax.ppermute(values, axis, [(i, i + 1) for i in range(lax.axis_size(axis) - 1)])


def down(values, axis):
    return lax.ppermute(values, axis, [(i + 1, i) for i in range(lax.axis_size(axis) - 1)])


def across(values):
    size = lax.axis_size("gy")
    pairs = [(i, i + 1) for i in range(1, size - 1, 2)]
    return lax.ppermute(values, "gy", pairs + [(j, i) for i, j in pairs])


def per_device(panel, tiles, codes):
    top = CELLS - 1
    own = panel[0, 0]
    odd = lax.axis_index("gy") % 2 == 1
    tiles = tiles.reshape(CELLS * SLOTS, SIDE, SIDE)
    codes = codes.reshape(CELLS * SLOTS)

    ends = jnp.concatenate([own[:1], own[top:]], axis=0)
    got = {"own": own}
    got["ends-"], got["ends+"] = up(ends, "gx"), down(ends, "gx")
    got["o"] = across(own)
    got["i"] = flip(own, "gy", 1)

    sides, tops, bottoms, mids = pack(
        got,
        [
            [("ends-", 0, 2), ("ends+", 0, 2)],
            [("own", top, 1), ("ends-", 1, 1), ("ends+", 1, 1)],
            [("own", 0, 1), ("ends-", 0, 1), ("ends+", 0, 1)],
            [("own", 1, 2)],
        ],
        after=(got["o"], got["i"]),
    )
    got["o2"] = across(sides)
    got["below2"], got["above2"] = up(tops, "gz"), down(bottoms, "gz")
    got["mids-"], got["mids+"] = up(mids, "gx"), down(mids, "gx")

    outer, tops, bottoms, inner = pack(
        got,
        [
            [("mids-", 0, 2), ("mids+", 0, 2), ("below2", 0, 1), ("above2", 0, 1)],
            [("o2", 1, 1), ("o2", 3, 1)],
            [("o2", 0, 1), ("o2", 2, 1)],
            [
                ("mids-", 0, 2), ("mids+", 0, 2), ("below2", 0, 3), ("above2", 0, 3),
                ("ends-", 0, 2), ("ends+", 0, 2),
            ],
        ],
    )
    got["o3"] = across(outer)
    got["below3"], got["above3"] = up(tops, "gz"), down(bottoms, "gz")
    got["i3"] = flip(inner, "gy", 1)

    filtered, gram = apply(odd, codes, tiles, got)
    devices = lax.axis_size("gx") * lax.axis_size("gy") * lax.axis_size("gz")
    bands, factor = factorise(summed(gram), filtered, CELLS * SIDE * devices)
    return bands.reshape(panel.shape), factor


def solution(mesh):
    in_specs = (
        P("gx", "gy", "gz", None, None),
        P("gx", "gy", "gz", None, None, None),
        P("gx", "gy", "gz", None),
    )
    out_specs = (P("gx", "gy", "gz", None, None), P())
    return jax.shard_map(
        per_device, mesh=mesh, in_specs=in_specs, out_specs=out_specs, check_vma=False
    )
```

```python
import functools

import jax
import jax.numpy as jnp
import numpy as np
from jax import lax
from jax.experimental import pallas as pl
from jax.experimental.pallas import tpu as pltpu
from jax.sharding import PartitionSpec as P

F32 = jnp.float32
BF16 = jnp.bfloat16
EXACT = lax.Precision.HIGHEST
CELLS = 4
SLOTS = 10
SIDE = 256
GROUP = 4
ROOM = 48
BLOCK = 64

STAGES = (
    (
        ("own", 4), ("i", 4), ("ends-", 2), ("ends+", 2),
        ("mids-", 2), ("mids+", 2), ("o2", 8), ("below2", 3), ("above2", 3),
    ),
    (("o3", 6), ("below3", 2), ("above3", 2), ("i3", 14)),
)


def place(column, dx, z):
    side = int(dx > 0)
    sign = "+" if dx > 0 else "-"
    last = int(z == CELLS - 1)
    inside = 0 <= z < CELLS
    mid = z in (1, 2)
    above = int(z > 0)
    outer = "above" if above else "below"
    if column == "own":
        if not inside:
            return (outer + "2", 0 if dx == 0 else 1 + side)
        if dx == 0:
            return ("own", z)
        return ("mids" + sign, z - 1) if mid else ("ends" + sign, last)
    if inside:
        if dx == 0:
            return ("o2", 4 + z) if column == "o" else ("i", z)
        if mid:
            return (column + "3", 2 * side + z - 1)
        return ("o2", 2 * side + last) if column == "o" else ("i3", 10 + 2 * side + last)
    if column == "o":
        return ("o3", 4 + above) if dx == 0 else (outer + "3", side)
    return ("i3", 4 + 3 * above + (0 if dx == 0 else 1 + side))


def lookup(buffers):
    start, total = {}, 0
    for name, count in buffers:
        start[name] = total
        total += count
    table = np.full((2, CELLS, 27), -1, np.int32)
    for parity in range(2):
        for cell in range(CELLS):
            for code in range(27):
                dx, dy, dz = code // 9 - 1, code // 3 % 3 - 1, code % 3 - 1
                inner = 1 if parity == 0 else -1
                column = "own" if dy == 0 else "i" if dy == inner else "o"
                name, at = place(column, dx, cell + dz)
                if name in start:
                    table[parity, cell, code] = start[name] + at
    return table.reshape(2, CELLS * 27)


def split(values):
    high = values.astype(BF16)
    return high, (values - high.astype(F32)).astype(BF16)


def product(a, b):
    ah, al = split(a)
    bh, bl = split(b)
    return jnp.dot(
        jnp.concatenate([ah, ah, al], axis=1),
        jnp.concatenate([bh, bl, bh], axis=0),
        preferred_element_type=F32,
    )


def pack_kernel(pieces, taken, given, *refs):
    sources, outs, sem = refs[:taken], refs[given:-1], refs[-1]
    copies = []
    for out, parts in zip(outs, pieces):
        start = 0
        for source, low, count in parts:
            copy = pltpu.make_async_copy(
                sources[source].at[pl.ds(low, count)],
                out.at[pl.ds(start, count)],
                sem.at[len(copies)],
            )
            copy.start()
            copies.append(copy)
            start += count
    for copy in copies:
        copy.wait()


def pack(got, payloads, after=()):
    names = sorted({name for parts in payloads for name, _, _ in parts})
    pieces = [[(names.index(name), low, count) for name, low, count in parts] for parts in payloads]
    anywhere = pl.BlockSpec(memory_space=pl.ANY)
    return pl.pallas_call(
        functools.partial(pack_kernel, pieces, len(names), len(names) + len(after)),
        out_shape=tuple(
            jax.ShapeDtypeStruct((sum(count for _, _, count in parts), SIDE, SIDE), F32)
            for parts in payloads
        ),
        in_specs=[anywhere] * (len(names) + len(after)),
        out_specs=(anywhere,) * len(payloads),
        scratch_shapes=[pltpu.SemaphoreType.DMA((sum(map(len, payloads)),))],
        compiler_params=pltpu.CompilerParams(vmem_limit_bytes=1 << 20),
        name="pack",
    )(*(got[name] for name in names), *after)


def listed(odd, table_ref, codes_ref, chosen, begin):
    taken = jnp.int32(0)
    for cell in range(CELLS):
        for at in range(cell * SLOTS, (cell + 1) * SLOTS):
            entry = table_ref[odd, 27 * cell + codes_ref[cell, at - cell * SLOTS]]

            @pl.when(entry >= 0)
            def _(at=at, cell=cell, entry=entry, taken=taken):
                chosen[0, taken] = jnp.int32(at)
                chosen[1, taken] = entry
                chosen[2, taken] = jnp.int32(cell)
                begin(at, taken)

            taken = taken + (entry >= 0).astype(jnp.int32)
    return taken


def multiply(taken, chosen, tile, window, arrived, total):
    for n in range(GROUP - 1):
        chosen[1, taken + n] = jnp.int32(0)
        chosen[2, taken + n] = jnp.int32(0)
        tile[taken + n] = jnp.zeros((SIDE, SIDE), F32)

    def group(g, carry):
        first = GROUP * g
        for n in range(GROUP):

            @pl.when(first + n < taken)
            def _(n=first + n):
                arrived(n)

        done = [product(tile[first + n], window[chosen[1, first + n]]) for n in range(GROUP)]
        for n in range(GROUP):
            total[chosen[2, first + n]] += done[n]
        return carry

    lax.fori_loop(0, (taken + GROUP - 1) // GROUP, group, 0)


def early_kernel(counts, table_ref, later_ref, codes_ref, tiles_ref, *rest):
    buffers, rest = rest[: len(counts)], rest[len(counts) :]
    out_ref, list_ref, window, tile, chosen, window_sem, tile_sem = rest
    copies, start = [], 0
    for n, (count, ref) in enumerate(zip(counts, buffers)):
        copy = pltpu.make_async_copy(ref, window.at[pl.ds(start, count)], window_sem.at[n])
        copy.start()
        copies.append(copy)
        start += count

    def fetch(at, n):
        return pltpu.make_async_copy(tiles_ref.at[at], tile.at[n], tile_sem.at[n])

    odd = lax.axis_index("gy") % 2
    taken = listed(odd, table_ref, codes_ref, chosen, lambda at, n: fetch(at, n).start())
    list_ref[0, ROOM - 1] = listed(odd, later_ref, codes_ref, list_ref, lambda at, n: None)
    for copy in copies:
        copy.wait()
    for cell in range(CELLS):
        out_ref[cell] = -0.5 * window[cell]
    multiply(taken, chosen, tile, window, lambda n: fetch(0, n).wait(), out_ref)


def late_kernel(counts, list_ref, tiles_ref, before_ref, *rest):
    buffers, rest = rest[: len(counts)], rest[len(counts) :]
    out_ref, gram_ref, total, window, tile, chosen, window_sem, tile_sem, sems = rest
    taken = list_ref[0, ROOM - 1]

    def fetch(at, n):
        return pltpu.make_async_copy(tiles_ref.at[at], tile.at[n], tile_sem.at[n])

    def begin(n, carry):
        entry = list_ref[1, n]
        chosen[1, n] = n
        chosen[2, n] = list_ref[2, n]
        fetch(list_ref[0, n], n).start()
        start = 0
        for count, ref in zip(counts, buffers):

            @pl.when((entry >= start) & (entry < start + count))
            def _(ref=ref, start=start):
                pltpu.make_async_copy(ref.at[entry - start], window.at[n], window_sem.at[n]).start()

            start += count
        return carry

    def arrived(n):
        fetch(0, n).wait()
        pltpu.make_async_copy(buffers[0].at[0], window.at[n], window_sem.at[n]).wait()

    lax.fori_loop(0, taken, begin, 0)
    before = pltpu.make_async_copy(before_ref, total, sems.at[CELLS])
    before.start()
    before.wait()
    multiply(taken, chosen, tile, window, arrived, total)
    copies = [
        pltpu.make_async_copy(total.at[cell], out_ref.at[cell], sems.at[cell]) for cell in range(CELLS)
    ]
    for copy in copies:
        copy.start()
    gram = jnp.zeros((SIDE, SIDE), F32)
    for cell in range(CELLS):
        high, low = split(total[cell])
        gram += lax.dot_general(
            jnp.concatenate([high, high, low], axis=0),
            jnp.concatenate([high, low, high], axis=0),
            (((0,), (0,)), ((), ())),
            preferred_element_type=F32,
        )
    gram_ref[...] = gram
    for copy in copies:
        copy.wait()


SMEM = pl.BlockSpec(memory_space=pltpu.SMEM)
FAR = pl.BlockSpec(memory_space=pltpu.HBM)
NEAR = pl.BlockSpec(memory_space=pltpu.VMEM)
SLOT_ROOM = CELLS * SLOTS + GROUP


def apply(codes, tiles, got):
    early, late = STAGES
    tables = [jnp.asarray(lookup(stage)) for stage in STAGES]
    counts = tuple(count for _, count in early)
    panel = jax.ShapeDtypeStruct((CELLS, SIDE, SIDE), F32)
    chosen = pltpu.SMEM((3, SLOT_ROOM), jnp.int32)
    tile = pltpu.VMEM((SLOT_ROOM, SIDE, SIDE), F32)
    params = pltpu.CompilerParams(vmem_limit_bytes=60 << 20)
    cost = pl.CostEstimate(
        flops=SLOTS * CELLS * 2 * SIDE**3, bytes_accessed=12 << 20, transcendentals=0
    )
    part, left = pl.pallas_call(
        functools.partial(early_kernel, counts),
        out_shape=(panel, jax.ShapeDtypeStruct((3, ROOM), jnp.int32)),
        in_specs=[SMEM, SMEM, SMEM, FAR] + [FAR] * len(counts),
        out_specs=(NEAR, SMEM),
        scratch_shapes=[
            pltpu.VMEM((sum(counts), SIDE, SIDE), F32),
            tile,
            chosen,
            pltpu.SemaphoreType.DMA((len(counts),)),
            pltpu.SemaphoreType.DMA((SLOT_ROOM,)),
        ],
        compiler_params=params,
        cost_estimate=cost,
        name="apply_early",
    )(*tables, codes, tiles, *(got[name] for name, _ in early))
    counts = tuple(count for _, count in late)
    return pl.pallas_call(
        functools.partial(late_kernel, counts),
        out_shape=(panel, jax.ShapeDtypeStruct((SIDE, SIDE), F32)),
        in_specs=[SMEM, FAR, FAR] + [FAR] * len(counts),
        out_specs=(FAR, NEAR),
        scratch_shapes=[
            pltpu.VMEM((CELLS, SIDE, SIDE), F32),
            tile,
            tile,
            chosen,
            pltpu.SemaphoreType.DMA((SLOT_ROOM,)),
            pltpu.SemaphoreType.DMA((SLOT_ROOM,)),
            pltpu.SemaphoreType.DMA((CELLS + 1,)),
        ],
        compiler_params=pltpu.CompilerParams(vmem_limit_bytes=59_400_000),
        cost_estimate=cost,
        name="apply_late",
    )(left, tiles, part, *(got[name] for name, _ in late))


def leaf(rows):
    rows = list(rows)
    at = lax.broadcasted_iota(jnp.int32, (8, 128), 0)
    count = len(rows)
    for b in range(count):
        rest = range(b, count)
        column = {
            (k, v): jnp.broadcast_to(rows[v][:, 8 * b + k : 8 * b + k + 1], (8, 128))
            for k in range(8)
            for v in rest
        }
        for j in range(8):
            scale = lax.rsqrt(jnp.broadcast_to(column[j, b][j : j + 1], (8, 128)))
            times = {v: column[j, v] * scale for v in rest}
            times[b] = jnp.where(at > j, times[b], 0.0)
            for k in range(j + 1, 8):
                pivot = jnp.broadcast_to(column[k, b][j : j + 1], (8, 128)) * scale
                for v in rest:
                    column[k, v] = column[k, v] - times[v] * pivot
            pivot = jnp.broadcast_to(rows[b][j : j + 1], (8, 128)) * scale
            for v in rest:
                if v > b:
                    rows[v] = rows[v] - times[v] * pivot
            rows[b] = jnp.where(at == j, pivot, rows[b] - times[b] * pivot)
    return rows


def factor_kernel(total, gram_ref, filtered_ref, bands_ref, factor_ref, work, filtered, bands, sems):
    fetch = pltpu.make_async_copy(filtered_ref, filtered, sems.at[CELLS])
    fetch.start()
    row = lax.broadcasted_iota(jnp.int32, (SIDE, SIDE), 0)
    col = lax.broadcasted_iota(jnp.int32, (SIDE, SIDE), 1)
    work[:, :SIDE] = gram_ref[...] * (1.0 / total)
    work[:, SIDE:] = (row == col).astype(F32)
    eye = (row == col)[:BLOCK, :BLOCK].astype(F32)
    for low in range(0, SIDE, BLOCK):
        high = low + BLOCK
        rows = pl.ds(low, BLOCK)
        block = jnp.concatenate([work[rows, low:high], eye], axis=1)
        done = jnp.concatenate(leaf([block[8 * v : 8 * v + 8] for v in range(BLOCK // 8)]), axis=0)
        solved = jnp.dot(done[:, BLOCK:], work[rows, :], precision=EXACT, preferred_element_type=F32)
        work[rows, :] = solved
        if high < SIDE:
            under = pl.ds(high, SIDE - high)
            work[under, :] = work[under, :] - lax.dot_general(
                solved[:, high:SIDE],
                solved,
                (((0,), (0,)), ((), ())),
                precision=EXACT,
                preferred_element_type=F32,
            )
    factor_ref[...] = jnp.where(row <= col, work[:, :SIDE], 0.0)
    high, low = split(jnp.where(row >= col, work[:, SIDE:], 0.0))
    right = jnp.concatenate([high, low, high], axis=1)
    fetch.wait()
    copies = []
    for cell in range(CELLS):
        fh, fl = split(filtered[cell])
        bands[cell] = lax.dot_general(
            jnp.concatenate([fh, fh, fl], axis=1),
            right,
            (((1,), (1,)), ((), ())),
            preferred_element_type=F32,
        )
        copies.append(pltpu.make_async_copy(bands.at[cell], bands_ref.at[cell], sems.at[cell]))
        copies[cell].start()
    for copy in copies:
        copy.wait()


def factorise(gram, filtered, total):
    vmem = pl.BlockSpec(memory_space=pltpu.VMEM)
    far = pl.BlockSpec(memory_space=pltpu.HBM)
    panel = (CELLS, SIDE, SIDE)
    return pl.pallas_call(
        functools.partial(factor_kernel, total),
        out_shape=(jax.ShapeDtypeStruct(panel, F32), jax.ShapeDtypeStruct((SIDE, SIDE), F32)),
        in_specs=[vmem, far],
        out_specs=(far, vmem),
        scratch_shapes=[
            pltpu.VMEM((SIDE, 2 * SIDE), F32),
            pltpu.VMEM(panel, F32),
            pltpu.VMEM(panel, F32),
            pltpu.SemaphoreType.DMA((CELLS + 1,)),
        ],
        compiler_params=pltpu.CompilerParams(vmem_limit_bytes=32 << 20),
        name="factorise",
    )(gram, filtered)


def flip(values, axis, bit):
    size = lax.axis_size(axis)
    return lax.ppermute(values, axis, [(i, i ^ bit) for i in range(size)])


def exchange(pieces, axes):
    return lax.all_to_all(pieces, axes, 0, 0).reshape(pieces.shape)


def summed(gram):
    plane = ("gx", "gy")
    peers, planes = lax.axis_size("gx") * lax.axis_size("gy"), lax.axis_size("gz")
    rows = exchange(gram.reshape(peers, SIDE // peers, SIDE), plane).sum(0)
    rows = exchange(jnp.broadcast_to(rows, (planes, *rows.shape)), "gz").sum(0)
    return exchange(jnp.broadcast_to(rows, (peers, *rows.shape)), plane).reshape(SIDE, SIDE)


def up(values, axis):
    return lax.ppermute(values, axis, [(i, i + 1) for i in range(lax.axis_size(axis) - 1)])


def down(values, axis):
    return lax.ppermute(values, axis, [(i + 1, i) for i in range(lax.axis_size(axis) - 1)])


def across(values):
    size = lax.axis_size("gy")
    pairs = [(i, i + 1) for i in range(1, size - 1, 2)]
    return lax.ppermute(values, "gy", pairs + [(j, i) for i, j in pairs])


def per_device(panel, tiles, codes):
    top = CELLS - 1
    own = panel[0, 0]
    tiles = tiles.reshape(CELLS * SLOTS, SIDE, SIDE)
    codes = codes[0, 0]

    first, last = own[:1], own[top:]
    ends = jnp.concatenate([first, last], axis=0)
    got = {"own": own, "first": first, "last": last, "between": own[1:top]}
    got["ends-"], got["ends+"] = up(ends, "gx"), down(ends, "gx")
    got["i"] = flip(own, "gy", 1)

    sides, tops, bottoms, mids = pack(
        got,
        [
            [("ends-", 0, 2), ("ends+", 0, 2), ("first", 0, 1), ("between", 0, 2), ("last", 0, 1)],
            [("last", 0, 1), ("ends-", 1, 1), ("ends+", 1, 1)],
            [("first", 0, 1), ("ends-", 0, 1), ("ends+", 0, 1)],
            [("between", 0, 2)],
        ],
        after=(got["i"],),
    )
    got["o2"] = across(sides)
    got["below2"], got["above2"] = up(tops, "gz"), down(bottoms, "gz")
    got["mids-"], got["mids+"] = up(mids, "gx"), down(mids, "gx")

    outer, tops, bottoms, inner = pack(
        got,
        [
            [("mids-", 0, 2), ("mids+", 0, 2), ("below2", 0, 1), ("above2", 0, 1)],
            [("o2", 1, 1), ("o2", 3, 1)],
            [("o2", 0, 1), ("o2", 2, 1)],
            [
                ("mids-", 0, 2), ("mids+", 0, 2), ("below2", 0, 3), ("above2", 0, 3),
                ("ends-", 0, 2), ("ends+", 0, 2),
            ],
        ],
    )
    got["o3"] = across(outer)
    got["below3"], got["above3"] = up(tops, "gz"), down(bottoms, "gz")
    got["i3"] = flip(inner, "gy", 1)

    filtered, gram = apply(codes, tiles, got)
    devices = lax.axis_size("gx") * lax.axis_size("gy") * lax.axis_size("gz")
    bands, factor = factorise(summed(gram), filtered, CELLS * SIDE * devices)
    return bands.reshape(panel.shape), factor


def solution(mesh):
    in_specs = (
        P("gx", "gy", "gz", None, None),
        P("gx", "gy", "gz", None, None, None),
        P("gx", "gy", "gz", None),
    )
    out_specs = (P("gx", "gy", "gz", None, None), P())
    return jax.shard_map(
        per_device, mesh=mesh, in_specs=in_specs, out_specs=out_specs, check_vma=False
    )
```

```python
import functools

import jax
import jax.numpy as jnp
import numpy as np
from jax import lax
from jax.experimental import pallas as pl
from jax.experimental.pallas import tpu as pltpu
from jax.sharding import PartitionSpec as P

F32 = jnp.float32
BF16 = jnp.bfloat16
EXACT = lax.Precision.HIGHEST
CELLS = 4
SLOTS = 10
SIDE = 256
GROUP = 4
ROOM = 48
BLOCK = 64

STAGES = (
    (
        ("own", 4), ("i", 4), ("ends-", 2), ("ends+", 2),
        ("mids-", 2), ("mids+", 2), ("o2", 8), ("below2", 3), ("above2", 3),
    ),
    (("o3", 6), ("below3", 2), ("above3", 2), ("i3", 14)),
)


def place(column, dx, z):
    side = int(dx > 0)
    sign = "+" if dx > 0 else "-"
    last = int(z == CELLS - 1)
    inside = 0 <= z < CELLS
    mid = z in (1, 2)
    above = int(z > 0)
    outer = "above" if above else "below"
    if column == "own":
        if not inside:
            return (outer + "2", 0 if dx == 0 else 1 + side)
        if dx == 0:
            return ("own", z)
        return ("mids" + sign, z - 1) if mid else ("ends" + sign, last)
    if inside:
        if dx == 0:
            return ("o2", 4 + z) if column == "o" else ("i", z)
        if mid:
            return (column + "3", 2 * side + z - 1)
        return ("o2", 2 * side + last) if column == "o" else ("i3", 10 + 2 * side + last)
    if column == "o":
        return ("o3", 4 + above) if dx == 0 else (outer + "3", side)
    return ("i3", 4 + 3 * above + (0 if dx == 0 else 1 + side))


def lookup(buffers):
    start, total = {}, 0
    for name, count in buffers:
        start[name] = total
        total += count
    table = np.full((2, CELLS, 27), -1, np.int32)
    for parity in range(2):
        for cell in range(CELLS):
            for code in range(27):
                dx, dy, dz = code // 9 - 1, code // 3 % 3 - 1, code % 3 - 1
                inner = 1 if parity == 0 else -1
                column = "own" if dy == 0 else "i" if dy == inner else "o"
                name, at = place(column, dx, cell + dz)
                if name in start:
                    table[parity, cell, code] = start[name] + at
    return table.reshape(2, CELLS * 27)


def split(values):
    high = values.astype(BF16)
    return high, (values - high.astype(F32)).astype(BF16)


def product(a, b):
    ah, al = split(a)
    bh, bl = split(b)
    return jnp.dot(
        jnp.concatenate([ah, ah, al], axis=1),
        jnp.concatenate([bh, bl, bh], axis=0),
        preferred_element_type=F32,
    )


def pack_kernel(pieces, taken, given, *refs):
    sources, outs, sem = refs[:taken], refs[given:-1], refs[-1]
    copies = []
    for out, parts in zip(outs, pieces):
        start = 0
        for source, low, count in parts:
            copy = pltpu.make_async_copy(
                sources[source].at[pl.ds(low, count)],
                out.at[pl.ds(start, count)],
                sem.at[len(copies)],
            )
            copy.start()
            copies.append(copy)
            start += count
    for copy in copies:
        copy.wait()


def pack(got, payloads, after=()):
    names = sorted({name for parts in payloads for name, _, _ in parts})
    pieces = [[(names.index(name), low, count) for name, low, count in parts] for parts in payloads]
    anywhere = pl.BlockSpec(memory_space=pl.ANY)
    return pl.pallas_call(
        functools.partial(pack_kernel, pieces, len(names), len(names) + len(after)),
        out_shape=tuple(
            jax.ShapeDtypeStruct((sum(count for _, _, count in parts), SIDE, SIDE), F32)
            for parts in payloads
        ),
        in_specs=[anywhere] * (len(names) + len(after)),
        out_specs=(anywhere,) * len(payloads),
        scratch_shapes=[pltpu.SemaphoreType.DMA((sum(map(len, payloads)),))],
        compiler_params=pltpu.CompilerParams(vmem_limit_bytes=1 << 20),
        name="pack",
    )(*(got[name] for name in names), *after)


def listed(odd, table_ref, codes_ref, chosen, begin):
    taken = jnp.int32(0)
    for cell in range(CELLS):
        for at in range(cell * SLOTS, (cell + 1) * SLOTS):
            entry = table_ref[odd, 27 * cell + codes_ref[cell, at - cell * SLOTS]]

            @pl.when(entry >= 0)
            def _(at=at, cell=cell, entry=entry, taken=taken):
                chosen[0, taken] = jnp.int32(at)
                chosen[1, taken] = entry
                chosen[2, taken] = jnp.int32(cell)
                begin(at, taken)

            taken = taken + (entry >= 0).astype(jnp.int32)
    return taken


def multiply(taken, chosen, tile, window, arrived, total):
    for n in range(GROUP - 1):
        chosen[1, taken + n] = jnp.int32(0)
        chosen[2, taken + n] = jnp.int32(0)
        tile[taken + n] = jnp.zeros((SIDE, SIDE), F32)

    def group(g, carry):
        first = GROUP * g
        for n in range(GROUP):

            @pl.when(first + n < taken)
            def _(n=first + n):
                arrived(n)

        done = [product(tile[first + n], window[chosen[1, first + n]]) for n in range(GROUP)]
        for n in range(GROUP):
            total[chosen[2, first + n]] += done[n]
        return carry

    lax.fori_loop(0, (taken + GROUP - 1) // GROUP, group, 0)


def early_kernel(counts, table_ref, later_ref, codes_ref, tiles_ref, *rest):
    buffers, rest = rest[: len(counts)], rest[len(counts) :]
    out_ref, list_ref, window, tile, chosen, window_sem, tile_sem = rest
    copies, start = [], 0
    for n, (count, ref) in enumerate(zip(counts, buffers)):
        copy = pltpu.make_async_copy(ref, window.at[pl.ds(start, count)], window_sem.at[n])
        copy.start()
        copies.append(copy)
        start += count

    def fetch(at, n):
        return pltpu.make_async_copy(tiles_ref.at[at], tile.at[n], tile_sem.at[n])

    odd = lax.axis_index("gy") % 2
    taken = listed(odd, table_ref, codes_ref, chosen, lambda at, n: fetch(at, n).start())
    list_ref[0, ROOM - 1] = listed(odd, later_ref, codes_ref, list_ref, lambda at, n: None)
    for copy in copies:
        copy.wait()
    for cell in range(CELLS):
        out_ref[cell] = -0.5 * window[cell]
    multiply(taken, chosen, tile, window, lambda n: fetch(0, n).wait(), out_ref)


def late_kernel(counts, list_ref, tiles_ref, before_ref, *rest):
    buffers, rest = rest[: len(counts)], rest[len(counts) :]
    out_ref, gram_ref, total, window, tile, chosen, window_sem, tile_sem, sems = rest
    taken = list_ref[0, ROOM - 1]

    def fetch(at, n):
        return pltpu.make_async_copy(tiles_ref.at[at], tile.at[n], tile_sem.at[n])

    def begin(n, carry):
        entry = list_ref[1, n]
        chosen[1, n] = n
        chosen[2, n] = list_ref[2, n]
        fetch(list_ref[0, n], n).start()
        start = 0
        for count, ref in zip(counts, buffers):

            @pl.when((entry >= start) & (entry < start + count))
            def _(ref=ref, start=start):
                pltpu.make_async_copy(ref.at[entry - start], window.at[n], window_sem.at[n]).start()

            start += count
        return carry

    def arrived(n):
        fetch(0, n).wait()
        pltpu.make_async_copy(buffers[0].at[0], window.at[n], window_sem.at[n]).wait()

    lax.fori_loop(0, taken, begin, 0)
    before = pltpu.make_async_copy(before_ref, total, sems.at[CELLS])
    before.start()
    before.wait()
    multiply(taken, chosen, tile, window, arrived, total)
    copies = [
        pltpu.make_async_copy(total.at[cell], out_ref.at[cell], sems.at[cell]) for cell in range(CELLS)
    ]
    for copy in copies:
        copy.start()
    gram = jnp.zeros((SIDE, SIDE), F32)
    for cell in range(CELLS):
        high, low = split(total[cell])
        gram += lax.dot_general(
            jnp.concatenate([high, high, low], axis=0),
            jnp.concatenate([high, low, high], axis=0),
            (((0,), (0,)), ((), ())),
            preferred_element_type=F32,
        )
    gram_ref[...] = gram
    for copy in copies:
        copy.wait()


SMEM = pl.BlockSpec(memory_space=pltpu.SMEM)
FAR = pl.BlockSpec(memory_space=pltpu.HBM)
NEAR = pl.BlockSpec(memory_space=pltpu.VMEM)
SLOT_ROOM = CELLS * SLOTS + GROUP


def apply(codes, tiles, got):
    early, late = STAGES
    tables = [jnp.asarray(lookup(stage)) for stage in STAGES]
    counts = tuple(count for _, count in early)
    panel = jax.ShapeDtypeStruct((CELLS, SIDE, SIDE), F32)
    chosen = pltpu.SMEM((3, SLOT_ROOM), jnp.int32)
    tile = pltpu.VMEM((SLOT_ROOM, SIDE, SIDE), F32)
    params = pltpu.CompilerParams(vmem_limit_bytes=60 << 20)
    cost = pl.CostEstimate(
        flops=SLOTS * CELLS * 2 * SIDE**3, bytes_accessed=12 << 20, transcendentals=0
    )
    part, left = pl.pallas_call(
        functools.partial(early_kernel, counts),
        out_shape=(panel, jax.ShapeDtypeStruct((3, ROOM), jnp.int32)),
        in_specs=[SMEM, SMEM, SMEM, FAR] + [FAR] * len(counts),
        out_specs=(NEAR, SMEM),
        scratch_shapes=[
            pltpu.VMEM((sum(counts), SIDE, SIDE), F32),
            tile,
            chosen,
            pltpu.SemaphoreType.DMA((len(counts),)),
            pltpu.SemaphoreType.DMA((SLOT_ROOM,)),
        ],
        compiler_params=params,
        cost_estimate=cost,
        name="apply_early",
    )(*tables, codes, tiles, *(got[name] for name, _ in early))
    counts = tuple(count for _, count in late)
    return pl.pallas_call(
        functools.partial(late_kernel, counts),
        out_shape=(panel, jax.ShapeDtypeStruct((SIDE, SIDE), F32)),
        in_specs=[SMEM, FAR, FAR] + [FAR] * len(counts),
        out_specs=(FAR, NEAR),
        scratch_shapes=[
            pltpu.VMEM((CELLS, SIDE, SIDE), F32),
            tile,
            tile,
            chosen,
            pltpu.SemaphoreType.DMA((SLOT_ROOM,)),
            pltpu.SemaphoreType.DMA((SLOT_ROOM,)),
            pltpu.SemaphoreType.DMA((CELLS + 1,)),
        ],
        compiler_params=pltpu.CompilerParams(vmem_limit_bytes=53_500_000),
        cost_estimate=cost,
        name="apply_late",
    )(left, tiles, part, *(got[name] for name, _ in late))


def leaf(rows):
    rows = list(rows)
    at = lax.broadcasted_iota(jnp.int32, (8, 128), 0)
    count = len(rows)
    for b in range(count):
        rest = range(b, count)
        column = {
            (k, v): jnp.broadcast_to(rows[v][:, 8 * b + k : 8 * b + k + 1], (8, 128))
            for k in range(8)
            for v in rest
        }
        for j in range(8):
            scale = lax.rsqrt(jnp.broadcast_to(column[j, b][j : j + 1], (8, 128)))
            times = {v: column[j, v] * scale for v in rest}
            times[b] = jnp.where(at > j, times[b], 0.0)
            for k in range(j + 1, 8):
                pivot = jnp.broadcast_to(column[k, b][j : j + 1], (8, 128)) * scale
                for v in rest:
                    column[k, v] = column[k, v] - times[v] * pivot
            pivot = jnp.broadcast_to(rows[b][j : j + 1], (8, 128)) * scale
            for v in rest:
                if v > b:
                    rows[v] = rows[v] - times[v] * pivot
            rows[b] = jnp.where(at == j, pivot, rows[b] - times[b] * pivot)
    return rows


def factor_kernel(total, gram_ref, filtered_ref, bands_ref, factor_ref, work, filtered, bands, sems):
    fetch = pltpu.make_async_copy(filtered_ref, filtered, sems.at[CELLS])
    fetch.start()
    row = lax.broadcasted_iota(jnp.int32, (SIDE, SIDE), 0)
    col = lax.broadcasted_iota(jnp.int32, (SIDE, SIDE), 1)
    work[:, :SIDE] = gram_ref[...] * (1.0 / total)
    work[:, SIDE:] = (row == col).astype(F32)
    eye = (row == col)[:BLOCK, :BLOCK].astype(F32)
    for low in range(0, SIDE, BLOCK):
        high = low + BLOCK
        rows = pl.ds(low, BLOCK)
        block = jnp.concatenate([work[rows, low:high], eye], axis=1)
        done = jnp.concatenate(leaf([block[8 * v : 8 * v + 8] for v in range(BLOCK // 8)]), axis=0)
        solved = jnp.dot(done[:, BLOCK:], work[rows, :], precision=EXACT, preferred_element_type=F32)
        work[rows, :] = solved
        if high < SIDE:
            under = pl.ds(high, SIDE - high)
            work[under, :] = work[under, :] - lax.dot_general(
                solved[:, high:SIDE],
                solved,
                (((0,), (0,)), ((), ())),
                precision=EXACT,
                preferred_element_type=F32,
            )
    factor_ref[...] = jnp.where(row <= col, work[:, :SIDE], 0.0)
    high, low = split(jnp.where(row >= col, work[:, SIDE:], 0.0))
    right = jnp.concatenate([high, low, high], axis=1)
    fetch.wait()
    copies = []
    for cell in range(CELLS):
        fh, fl = split(filtered[cell])
        bands[cell] = lax.dot_general(
            jnp.concatenate([fh, fh, fl], axis=1),
            right,
            (((1,), (1,)), ((), ())),
            preferred_element_type=F32,
        )
        copies.append(pltpu.make_async_copy(bands.at[cell], bands_ref.at[cell], sems.at[cell]))
        copies[cell].start()
    for copy in copies:
        copy.wait()


def factorise(gram, filtered, total):
    vmem = pl.BlockSpec(memory_space=pltpu.VMEM)
    far = pl.BlockSpec(memory_space=pltpu.HBM)
    panel = (CELLS, SIDE, SIDE)
    return pl.pallas_call(
        functools.partial(factor_kernel, total),
        out_shape=(jax.ShapeDtypeStruct(panel, F32), jax.ShapeDtypeStruct((SIDE, SIDE), F32)),
        in_specs=[vmem, far],
        out_specs=(far, vmem),
        scratch_shapes=[
            pltpu.VMEM((SIDE, 2 * SIDE), F32),
            pltpu.VMEM(panel, F32),
            pltpu.VMEM(panel, F32),
            pltpu.SemaphoreType.DMA((CELLS + 1,)),
        ],
        compiler_params=pltpu.CompilerParams(vmem_limit_bytes=32 << 20),
        name="factorise",
    )(gram, filtered)


def flip(values, axis, bit):
    size = lax.axis_size(axis)
    return lax.ppermute(values, axis, [(i, i ^ bit) for i in range(size)])


def exchange(pieces, axes):
    return lax.all_to_all(pieces, axes, 0, 0).reshape(pieces.shape)


def summed(gram):
    plane = ("gx", "gy")
    peers, planes = lax.axis_size("gx") * lax.axis_size("gy"), lax.axis_size("gz")
    rows = exchange(gram.reshape(peers, SIDE // peers, SIDE), plane).sum(0)
    rows = exchange(jnp.broadcast_to(rows, (planes, *rows.shape)), "gz").sum(0)
    return exchange(jnp.broadcast_to(rows, (peers, *rows.shape)), plane).reshape(SIDE, SIDE)


def up(values, axis):
    return lax.ppermute(values, axis, [(i, i + 1) for i in range(lax.axis_size(axis) - 1)])


def down(values, axis):
    return lax.ppermute(values, axis, [(i + 1, i) for i in range(lax.axis_size(axis) - 1)])


def across(values):
    size = lax.axis_size("gy")
    pairs = [(i, i + 1) for i in range(1, size - 1, 2)]
    return lax.ppermute(values, "gy", pairs + [(j, i) for i, j in pairs])


def per_device(panel, tiles, codes):
    top = CELLS - 1
    own = panel[0, 0]
    tiles = tiles.reshape(CELLS * SLOTS, SIDE, SIDE)
    codes = codes[0, 0]

    first, last = own[:1], own[top:]
    ends = jnp.concatenate([first, last], axis=0)
    got = {"own": own, "first": first, "last": last, "between": own[1:top]}
    got["ends-"], got["ends+"] = up(ends, "gx"), down(ends, "gx")
    got["i"] = flip(own, "gy", 1)

    sides, tops, bottoms, mids = pack(
        got,
        [
            [("ends-", 0, 2), ("ends+", 0, 2), ("first", 0, 1), ("between", 0, 2), ("last", 0, 1)],
            [("last", 0, 1), ("ends-", 1, 1), ("ends+", 1, 1)],
            [("first", 0, 1), ("ends-", 0, 1), ("ends+", 0, 1)],
            [("between", 0, 2)],
        ],
        after=(got["i"],),
    )
    got["o2"] = across(sides)
    got["below2"], got["above2"] = up(tops, "gz"), down(bottoms, "gz")
    got["mids-"], got["mids+"] = up(mids, "gx"), down(mids, "gx")

    outer, tops, bottoms, inner = pack(
        got,
        [
            [("mids-", 0, 2), ("mids+", 0, 2), ("below2", 0, 1), ("above2", 0, 1)],
            [("o2", 1, 1), ("o2", 3, 1)],
            [("o2", 0, 1), ("o2", 2, 1)],
            [
                ("mids-", 0, 2), ("mids+", 0, 2), ("below2", 0, 3), ("above2", 0, 3),
                ("ends-", 0, 2), ("ends+", 0, 2),
            ],
        ],
    )
    got["o3"] = across(outer)
    got["below3"], got["above3"] = up(tops, "gz"), down(bottoms, "gz")
    got["i3"] = flip(inner, "gy", 1)

    filtered, gram = apply(codes, tiles, got)
    devices = lax.axis_size("gx") * lax.axis_size("gy") * lax.axis_size("gz")
    bands, factor = factorise(summed(gram), filtered, CELLS * SIDE * devices)
    return bands.reshape(panel.shape), factor


def solution(mesh):
    in_specs = (
        P("gx", "gy", "gz", None, None),
        P("gx", "gy", "gz", None, None, None),
        P("gx", "gy", "gz", None),
    )
    out_specs = (P("gx", "gy", "gz", None, None), P())
    return jax.shard_map(
        per_device, mesh=mesh, in_specs=in_specs, out_specs=out_specs, check_vma=False
    )
```
